32 devices in a mesh: band: 32 (over z, y, x, core).
Axes of the slice: x: 2, y: 2, z: 4, core: 2. Of those that a mesh axis runs over, the one named last changes fastest.
Arguments:
- grid_input: bfloat16 [227, 32768], P(None, 'band'), may hold values from -6 to 6
- mesh_init: bfloat16 [8192, 512], P('band'), may hold values from -6 to 6
- cotangent: bfloat16 [8192, 512], P('band'), may hold values from -6 to 6
- grid_lists: int32 [64, 256], P('band'), may hold values from 0 to 1023
- encoder_source: int32 [49152], P('band'), may hold values from 0 to 1535
- encoder_target: int32 [49152], P('band'), may hold values from 0 to 255
- mesh_lists: int32 [1024, 2], P('band'), may hold values from 0 to 255
- mesh_source: int32 [65536], P('band'), may hold values from 0 to 319
- mesh_target: int32 [65536], P('band'), may hold values from 0 to 255
- w_embed: bfloat16 [227, 512], replicated, may hold values from -0.375 to 0.375
- w_source: bfloat16 [512, 512], replicated, may hold values from -0.25 to 0.25
- w_target: bfloat16 [512, 512], replicated, may hold values from -0.25 to 0.25
- w_node: bfloat16 [512, 512], replicated, may hold values from -0.109375 to 0.109375
- w_sender: bfloat16 [512, 512], replicated, may hold values from -0.25 to 0.25
- w_receiver: bfloat16 [512, 512], replicated, may hold values from -0.25 to 0.25
- w_update: bfloat16 [512, 512], replicated, may hold values from -0.09375 to 0.09375
Outputs:
- mesh_out: bfloat16 [8192, 512], P('band')
- grad_grid: bfloat16 [227, 32768], P(None, 'band')
- grad_mesh: bfloat16 [8192, 512], P('band')
The draws below stay inside these ranges and needn't reach their ends.
Inputs may be any that keep to these rules, and one draw needn't show every extreme that they name: `grid_lists`: local grid row of the sending band. `encoder_source`: row of the band's grid source table. `mesh_lists`: local mesh node of the sending patch. `mesh_source`: row of the patch's mesh source table.
All inputs are finite; a program needn't handle non-finite values.
Results may differ from the reference program's by a relative error of at most 0.025.
Values may be sent and summed in bfloat16 or wider, within the bound.
A program may use at most 128 MiB of HBM per device.

```python
import jax
import jax.numpy as jnp
from jax import lax

D = 512
C_IN = 227
G_DEV = 1024
M_DEV = 256
CAPM = 2
CAPG = 256
ENC_DEV = 1536
PROC_DEV = 2048
BANDS = 32
GRID = 32768
MESH = 8192
GTAB = 1536
MTAB = 320
N_BAND = 32


def set_ends(values, stream_key, smallest, largest):
    longest = values.shape.index(max(values.shape))
    spots = []
    for shift in (0, 1):
        where = [jax.random.randint(jax.random.fold_in(stream_key, axis), (), 0, length) for axis, length in enumerate(values.shape)]
        where[longest] = (where[longest] + shift) % values.shape[longest]
        spots.append(tuple(where))
    return values.at[spots[0]].set(smallest).at[spots[1]].set(largest)


def steps_of(key, dims, pieces, low, high):
    loudness, own = 1.0, jax.random.fold_in(key, 6)
    for axis_at, blocks in pieces:
        heights = jnp.exp(jax.random.uniform(jax.random.fold_in(own, axis_at), (blocks,), jnp.float32, low / len(pieces), high / len(pieces)))
        loudness = loudness * jnp.repeat(heights, dims[axis_at] // blocks).reshape([-1 if axis == axis_at else 1 for axis in range(len(dims))])
    return loudness


def bell_draw(rng, shape, spread, bound, split=(), dtype=jnp.bfloat16):
    values = jax.random.normal(rng, shape, jnp.float32) * spread
    if len(split) > 0:
        values = steps_of(rng, shape, split, -0.22, 0.18) * values
    return jnp.clip(values, min=-bound, max=bound).astype(dtype)


def setup_inputs(seed: int = 0) -> dict:
    seeds = jax.random.split(jax.random.key(seed), 17)
    grid_input = bell_draw(seeds[0], (C_IN, GRID), 1.0, 6.0, ((1, 32),))
    mesh_init = bell_draw(seeds[1], (MESH, D), 1.0, 6.0, ((0, 32),))
    cotangent = bell_draw(seeds[2], (MESH, D), 1.0, 6.0, ((0, 32),))
    grid_lists = set_ends(jax.random.randint(seeds[3], (2 * BANDS, CAPG), 0, G_DEV), jax.random.fold_in(seeds[3], 1), 0, G_DEV - 1).astype(jnp.int32)
    encoder_source = set_ends(jax.random.randint(seeds[4], (ENC_DEV * BANDS,), 0, GTAB), jax.random.fold_in(seeds[4], 1), 0, GTAB - 1).astype(jnp.int32)
    encoder_target = set_ends(jax.random.randint(seeds[5], (ENC_DEV * BANDS,), 0, M_DEV), jax.random.fold_in(seeds[5], 1), 0, M_DEV - 1).astype(jnp.int32)
    mesh_lists = set_ends(jax.random.randint(seeds[6], (BANDS * BANDS, CAPM), 0, M_DEV), jax.random.fold_in(seeds[6], 1), 0, M_DEV - 1).astype(jnp.int32)
    mesh_source = set_ends(jax.random.randint(seeds[7], (PROC_DEV * BANDS,), 0, MTAB), jax.random.fold_in(seeds[7], 1), 0, MTAB - 1).astype(jnp.int32)
    mesh_target = set_ends(jax.random.randint(seeds[8], (PROC_DEV * BANDS,), 0, M_DEV), jax.random.fold_in(seeds[8], 1), 0, M_DEV - 1).astype(jnp.int32)
    w_embed = bell_draw(seeds[9], (C_IN, D), C_IN ** -0.5, 0.375)
    w_source = bell_draw(seeds[10], (D, D), D ** -0.5, 0.25)
    w_target = bell_draw(seeds[11], (D, D), D ** -0.5, 0.25)
    w_node = bell_draw(seeds[12], (D, D), (D * ENC_DEV // M_DEV) ** -0.5, 0.109375)
    w_sender = bell_draw(seeds[13], (D, D), D ** -0.5, 0.25)
    w_receiver = bell_draw(seeds[14], (D, D), D ** -0.5, 0.25)
    w_update = bell_draw(seeds[15], (D, D), (D * PROC_DEV // M_DEV) ** -0.5, 0.09375)
    return dict(grid_input=grid_input, mesh_init=mesh_init, cotangent=cotangent, grid_lists=grid_lists, encoder_source=encoder_source, encoder_target=encoder_target, mesh_lists=mesh_lists, mesh_source=mesh_source, mesh_target=mesh_target, w_embed=w_embed, w_source=w_source, w_target=w_target, w_node=w_node, w_sender=w_sender, w_receiver=w_receiver, w_update=w_update)


def rounded(values):
    return lax.optimization_barrier(values.astype(jnp.bfloat16)).astype(jnp.float32)

def aggregate(items):
    table_part, proj_part, source_index, target_index = items
    message = jax.nn.silu(table_part[source_index] + proj_part[target_index]).astype(jnp.bfloat16)
    return jax.ops.segment_sum(message.astype(jnp.float32), target_index, num_segments=M_DEV)

def pick_rows(table_rows, index_list):
    return table_rows[index_list]

def reference(grid_input, mesh_init, cotangent, grid_lists, encoder_source, encoder_target, mesh_lists, mesh_source, mesh_target, w_embed, w_source, w_target, w_node, w_sender, w_receiver, w_update):
    band_count = N_BAND
    picker = jax.vmap(pick_rows)

    def forward(grid_values, mesh_values):
        hidden = jax.nn.silu(lax.dot_general(grid_values, w_embed, (((0,), (0,)), ((), ())), preferred_element_type=jnp.float32)).astype(jnp.bfloat16)
        source_all = rounded(jnp.dot(hidden, w_source, preferred_element_type=jnp.float32)).reshape(band_count, G_DEV, D)
        send_lists = grid_lists.reshape(band_count, 2, CAPG)
        to_lower = picker(source_all, send_lists[:, 0])
        to_upper = picker(source_all, send_lists[:, 1])
        nothing = jnp.zeros((1, CAPG, D), jnp.float32)
        from_lower = jnp.concatenate([nothing, to_upper[:-1]], axis=0)
        from_upper = jnp.concatenate([to_lower[1:], nothing], axis=0)
        grid_table = jnp.concatenate([source_all, from_lower, from_upper], axis=1)
        mesh_float = mesh_values.astype(jnp.float32)
        target_proj = jnp.dot(mesh_float.astype(jnp.bfloat16), w_target, preferred_element_type=jnp.float32).reshape(band_count, M_DEV, D)
        enc_sum = lax.map(aggregate, (grid_table, target_proj, encoder_source.reshape(band_count, ENC_DEV), encoder_target.reshape(band_count, ENC_DEV)))
        enc_sum = enc_sum.reshape(band_count * M_DEV, D)
        latent = rounded(mesh_float + jax.nn.silu(jnp.dot(enc_sum.astype(jnp.bfloat16), w_node, preferred_element_type=jnp.float32)))
        sender_rows = rounded(jnp.dot(latent.astype(jnp.bfloat16), w_sender, preferred_element_type=jnp.float32)).reshape(band_count, M_DEV, D)
        sent = picker(sender_rows, mesh_lists.reshape(band_count, band_count * CAPM)).reshape(band_count, band_count, CAPM, D)
        received = jnp.transpose(sent, (1, 0, 2, 3)).reshape(band_count, band_count * CAPM, D)
        mesh_table = jnp.concatenate([sender_rows, received], axis=1)
        receiver_proj = jnp.dot(latent.astype(jnp.bfloat16), w_receiver, preferred_element_type=jnp.float32).reshape(band_count, M_DEV, D)
        proc_sum = lax.map(aggregate, (mesh_table, receiver_proj, mesh_source.reshape(band_count, PROC_DEV), mesh_target.reshape(band_count, PROC_DEV)))
        proc_sum = proc_sum.reshape(band_count * M_DEV, D)
        update = jax.nn.silu(jnp.dot(proc_sum.astype(jnp.bfloat16), w_update, preferred_element_type=jnp.float32))
        return (latent + update).astype(jnp.bfloat16)
    mesh_out, pullback = jax.vjp(forward, grid_input, mesh_init)
    grad_grid, grad_mesh = pullback(cotangent)
    return (mesh_out, grad_grid, grad_mesh)
```

```python
import jax
import jax.numpy as jnp
from jax import lax
from jax.sharding import PartitionSpec as P


def padded(block, sides, width):
    for axis, dim in sides:
        count = lax.axis_size(axis)
        forward = [(i, i + 1) for i in range(count - 1)]
        backward = [(target, source) for source, target in forward]
        low = lax.ppermute(
            lax.slice_in_dim(block, block.shape[dim] - width, None, axis=dim), axis, forward
        )
        high = lax.ppermute(lax.slice_in_dim(block, 0, width, axis=dim), axis, backward)
        block = jnp.concatenate([low, block, high], axis=dim)
    return block


def rounded(values):
    return lax.optimization_barrier(values.astype(jnp.bfloat16)).astype(jnp.float32)


def indicator(indices, count):
    return (indices[:, None] == jnp.arange(count, dtype=jnp.int32)[None, :]).astype(jnp.bfloat16)


def carry_rows(selector, values, axis):
    dims = (((axis,), (0,)), ((), ()))
    return lax.dot_general(selector, values.astype(jnp.bfloat16), dims, preferred_element_type=jnp.float32)


def local(
    grid_input,
    mesh_init,
    cotangent,
    grid_lists,
    encoder_source,
    encoder_target,
    mesh_lists,
    mesh_source,
    mesh_target,
    w_embed,
    w_source,
    w_target,
    w_node,
    w_sender,
    w_receiver,
    w_update,
):
    band_count = lax.axis_size("band")
    grid_count = grid_input.shape[1]
    node_count = mesh_init.shape[0]
    latent_width = mesh_init.shape[1]
    grid_slots = grid_lists.shape[1]
    mesh_slots = mesh_lists.shape[1]

    def embedding(grid_values):
        hidden = jax.nn.silu(
            lax.dot_general(
                grid_values, w_embed, (((0,), (0,)), ((), ())), preferred_element_type=jnp.float32
            )
        ).astype(jnp.bfloat16)
        return rounded(jnp.dot(hidden, w_source, preferred_element_type=jnp.float32))

    source_rows, embed_pull = jax.vjp(embedding, grid_input)
    source_half = source_rows.astype(jnp.bfloat16)
    list_rows = jnp.concatenate([grid_lists[0], grid_lists[1]], axis=0)
    list_select = indicator(list_rows, grid_count)
    outgoing = jnp.dot(list_select, source_half, preferred_element_type=jnp.float32).astype(
        jnp.bfloat16
    )
    extended = padded(outgoing, (("band", 0),), grid_slots)
    grid_table = jnp.concatenate(
        [source_half, extended[:grid_slots], extended[3 * grid_slots :]], axis=0
    )
    source_select = indicator(encoder_source, grid_table.shape[0])
    edge_source = jnp.dot(source_select, grid_table, preferred_element_type=jnp.float32)
    enc_onehot = (
        jnp.arange(node_count, dtype=jnp.int32)[:, None] == encoder_target[None, :]
    ).astype(jnp.bfloat16)
    proc_onehot = (jnp.arange(node_count, dtype=jnp.int32)[:, None] == mesh_target[None, :]).astype(
        jnp.bfloat16
    )
    mesh_float = mesh_init.astype(jnp.float32)

    def target_side(mesh_values):
        return jnp.dot(
            mesh_values.astype(jnp.bfloat16), w_target, preferred_element_type=jnp.float32
        )

    target_proj, target_pull = jax.vjp(target_side, mesh_float)
    edge_target = carry_rows(enc_onehot, target_proj, 0)

    def encoder(source_values, target_values, mesh_values):
        message = jax.nn.silu(source_values + target_values).astype(jnp.bfloat16)
        summed = jnp.dot(enc_onehot, message, preferred_element_type=jnp.float32)
        return rounded(
            mesh_values
            + jax.nn.silu(
                jnp.dot(summed.astype(jnp.bfloat16), w_node, preferred_element_type=jnp.float32)
            )
        )

    latent, encode_pull = jax.vjp(encoder, edge_source, edge_target, mesh_float)

    def projection(latent_values):
        return rounded(
            jnp.dot(
                latent_values.astype(jnp.bfloat16), w_sender, preferred_element_type=jnp.float32
            )
        )

    sender_rows, project_pull = jax.vjp(projection, latent)
    sender_half = sender_rows.astype(jnp.bfloat16)
    flat_lists = mesh_lists.reshape(-1)
    mesh_select = indicator(flat_lists, node_count)
    outbound = jnp.dot(mesh_select, sender_half, preferred_element_type=jnp.float32).astype(
        jnp.bfloat16
    )
    outbound = outbound.reshape(band_count, mesh_slots, latent_width)
    received = lax.all_to_all(outbound, "band", split_axis=0, concat_axis=0, tiled=True)
    received = received.reshape(band_count * mesh_slots, latent_width)
    mesh_table = jnp.concatenate([sender_half, received], axis=0)
    proc_select = indicator(mesh_source, mesh_table.shape[0])
    edge_sender = jnp.dot(proc_select, mesh_table, preferred_element_type=jnp.float32)

    def receiver_side(latent_values):
        return jnp.dot(
            latent_values.astype(jnp.bfloat16), w_receiver, preferred_element_type=jnp.float32
        )

    receiver_proj, receiver_pull = jax.vjp(receiver_side, latent)
    edge_receiver = carry_rows(proc_onehot, receiver_proj, 0)

    def processor(sender_values, receiver_values, latent_values):
        message = jax.nn.silu(sender_values + receiver_values).astype(jnp.bfloat16)
        summed = jnp.dot(proc_onehot, message, preferred_element_type=jnp.float32)
        update = jax.nn.silu(
            jnp.dot(summed.astype(jnp.bfloat16), w_update, preferred_element_type=jnp.float32)
        )
        return (latent_values + update).astype(jnp.bfloat16)

    mesh_out, process_pull = jax.vjp(processor, edge_sender, edge_receiver, latent)
    grad_edge_sender, grad_edge_receiver, grad_latent_direct = process_pull(cotangent)
    grad_table = carry_rows(proc_select, grad_edge_sender, 0)
    (grad_latent_receiver,) = receiver_pull(carry_rows(proc_onehot, grad_edge_receiver, 1))
    grad_received = grad_table[node_count:].reshape(band_count, mesh_slots, latent_width)
    returned_mesh = lax.all_to_all(
        grad_received.astype(jnp.bfloat16), "band", split_axis=0, concat_axis=0, tiled=True
    ).astype(grad_received.dtype)
    grad_sender = grad_table[:node_count] + carry_rows(
        mesh_select, returned_mesh.reshape(-1, latent_width), 0
    )
    (grad_latent_project,) = project_pull(grad_sender)
    grad_latent = grad_latent_direct + grad_latent_receiver + grad_latent_project
    grad_edge_source, grad_edge_target, grad_mesh_direct = encode_pull(grad_latent)
    (grad_mesh_target,) = target_pull(carry_rows(enc_onehot, grad_edge_target, 1))
    grad_mesh = (grad_mesh_direct + grad_mesh_target).astype(jnp.bfloat16)
    grad_grid_table = carry_rows(source_select, grad_edge_source, 0)
    grad_from_lower = grad_grid_table[grid_count : grid_count + grid_slots]
    grad_from_upper = grad_grid_table[grid_count + grid_slots :]
    returned_grid = padded(
        jnp.concatenate([grad_from_lower, grad_from_upper], axis=0).astype(jnp.bfloat16),
        (("band", 0),),
        grid_slots,
    ).astype(jnp.float32)
    grad_lists = jnp.concatenate(
        [returned_grid[:grid_slots], returned_grid[3 * grid_slots :]], axis=0
    )
    grad_source = grad_grid_table[:grid_count] + carry_rows(list_select, grad_lists, 0)
    (grad_grid,) = embed_pull(grad_source)
    return (mesh_out, grad_grid, grad_mesh)


def solution(mesh):
    placed = (
        P(None, "band"),
        P("band", None),
        P("band", None),
        P("band", None),
        P("band"),
        P("band"),
        P("band", None),
        P("band"),
        P("band"),
        P(),
        P(),
        P(),
        P(),
        P(),
        P(),
        P(),
    )
    return jax.shard_map(
        local,
        mesh=mesh,
        in_specs=placed,
        out_specs=(P("band", None), P(None, "band"), P("band", None)),
        check_vma=False,
    )
```

```python
import functools

import jax
import jax.numpy as jnp
from jax import lax
from jax.experimental import pallas as pl
from jax.experimental.pallas import tpu as pltpu
from jax.sharding import PartitionSpec as P

F32 = jnp.float32
BF16 = jnp.bfloat16
MESH = pl.DeviceIdType.MESH
LANES = 128
TILE = 512


def nn(left, right):
    return jnp.dot(left, right, preferred_element_type=F32)


def nt(left, right):
    return lax.dot_general(left, right, (((1,), (1,)), ((), ())), preferred_element_type=F32)


def tn(left, right):
    return lax.dot_general(left, right, (((0,), (0,)), ((), ())), preferred_element_type=F32)


def gate(values):
    sigmoid = 0.5 * jnp.tanh(0.5 * values) + 0.5
    out = values * sigmoid
    return out, sigmoid + out - out * sigmoid


def pick(column, base, width, shift=0):
    lane = lax.broadcasted_iota(jnp.int32, column.shape, 1)
    parts = [
        jnp.where(column == lax.shift_right_logical(lane + k, shift) + base, 1.0, 0.0).astype(BF16)
        for k in range(0, width, LANES)
    ]
    return jnp.concatenate(parts, axis=1)


def spread(index_ref, first, groups, base, rows, shift=0):
    row = lax.broadcasted_iota(jnp.int32, (rows, LANES), 0)
    row = lax.shift_right_logical(row, shift) + base
    parts = [
        jnp.where(index_ref[g : g + 1, :] == row, 1.0, 0.0).astype(BF16)
        for g in range(first, first + groups)
    ]
    return jnp.concatenate(parts, axis=1)


def block_rows(shape, blocks):
    return lax.broadcasted_iota(jnp.int32, shape, 0) & (blocks - 1)


def packed(full, blocks):
    which = block_rows((full.shape[0], LANES), blocks)
    out = full[:, :LANES]
    for c in range(1, blocks):
        out = jnp.where(which == c, full[:, c * LANES : (c + 1) * LANES], out)
    return out


def unpacked(part, blocks):
    which = block_rows(part.shape, blocks)
    return jnp.concatenate(
        [jnp.where(which == c, part, 0.0).astype(BF16) for c in range(blocks)], axis=1
    )


def kernel(
    n,
    at,
    enc_source_ref,
    enc_target_ref,
    proc_source_ref,
    proc_target_ref,
    lists_ref,
    mesh_lists_ref,
    grid_in,
    mesh_ref,
    cot_ref,
    embed_in,
    w_source,
    w_target,
    w_node,
    w_sender,
    w_receiver,
    w_update,
    out_ref,
    grad_grid_ref,
    grad_mesh_ref,
    index_ref,
    column,
    grid_ref,
    w_embed,
    list_hot,
    table,
    halo,
    halo_send,
    halo_recv,
    back,
    back_send,
    pre,
    edge,
    grad_part,
    slope_grid,
    slope_halo,
    slope_enc,
    slope_proc,
    pair,
    hot_halo,
    hot_enc,
    row_enc,
    row_halo,
    hot_far,
    hot_proc,
    row_proc,
    row_far,
    hot_lists,
    slab_send,
    slab_recv,
    turn_send,
    turn_recv,
    halo_sems,
    slab_sems,
):
    me = lax.axis_index("band")
    channels, grid_count = grid_in.shape
    nodes, width = mesh_ref.shape
    half = halo.shape[0] // 2
    enc = slope_enc.shape[0]
    proc = slope_proc.shape[0]
    slots = mesh_lists_ref.shape[0]
    blocks = width // LANES
    shift = blocks.bit_length() - 1
    per = slots * blocks
    slabs = n * per
    deep = grid_ref.shape[0]

    def exchange(source, target, k, kind):
        device = lax.rem(me + (n - 1 if k == 0 else 1), n)
        return pltpu.make_async_remote_copy(
            src_ref=source.at[pl.ds(k * half, half)],
            dst_ref=target.at[pl.ds((1 - k) * half, half)],
            send_sem=halo_sems.at[kind, 0, k],
            recv_sem=halo_sems.at[kind, 1, k],
            device_id=(device,),
            device_id_type=MESH,
        )

    def exchange_start(source, target, kind):
        @pl.when(me > 0)
        def _():
            exchange(source, target, 0, kind).start()

        @pl.when(me < n - 1)
        def _():
            exchange(source, target, 1, kind).start()

    def exchange_wait(source, target, kind):
        @pl.when(me < n - 1)
        def _():
            exchange(source, target, 0, kind).wait_recv()
            exchange(source, target, 1, kind).wait_send()

        @pl.when(me > 0)
        def _():
            exchange(source, target, 1, kind).wait_recv()
            exchange(source, target, 0, kind).wait_send()

    def scatter_start(source, target, kind):
        def send(k, carry):
            other = lax.rem(me + k, n)
            pltpu.make_async_remote_copy(
                src_ref=source.at[other],
                dst_ref=target.at[me],
                send_sem=slab_sems.at[kind, 0],
                recv_sem=slab_sems.at[kind, 1],
                device_id=(other,),
                device_id_type=MESH,
            ).start()
            return carry

        lax.fori_loop(1, n, send, 0)

    def scatter_wait(source, target, kind):
        whole_source = source.at[pl.ds(0, n - 1)]
        whole_target = target.at[pl.ds(0, n - 1)]
        pltpu.make_async_copy(whole_source, whole_target, slab_sems.at[kind, 0]).wait()
        pltpu.make_async_copy(whole_source, whole_target, slab_sems.at[kind, 1]).wait()

    @pl.when(me == 0)
    def _():
        halo_recv[pl.ds(0, half), :] = jnp.zeros((half, deep), BF16)
        back[pl.ds(0, half), :] = jnp.zeros((half, deep), BF16)

    @pl.when(me == n - 1)
    def _():
        halo_recv[pl.ds(half, half), :] = jnp.zeros((half, deep), BF16)
        back[pl.ds(half, half), :] = jnp.zeros((half, deep), BF16)

    barrier = pltpu.get_barrier_semaphore()

    def greet(k, carry):
        pl.semaphore_signal(
            barrier, inc=1, device_id=(lax.rem(me + k, n),), device_id_type=MESH
        )
        return carry

    lax.fori_loop(1, n, greet, 0)

    index_ref[...] = jnp.zeros_like(index_ref)
    for name, ref in (
        ("enc_source", enc_source_ref),
        ("enc_target", enc_target_ref),
        ("proc_source", proc_source_ref),
        ("proc_target", proc_target_ref),
    ):
        for g in range(ref.shape[1] // LANES):
            index_ref[at[name] + g : at[name] + g + 1, :] = ref[:, g * LANES : (g + 1) * LANES]
    each = half // LANES
    for g in range(2 * each):
        index_ref[at["lists"] + g : at["lists"] + g + 1, :] = lists_ref[
            g // each : g // each + 1, g % each * LANES : (g % each + 1) * LANES
        ]
    for j in range(slots):
        index_ref[at["mesh_lists"] + j : at["mesh_lists"] + j + 1, 0:n] = mesh_lists_ref[
            j : j + 1, :
        ]
    turned = jnp.transpose(index_ref[...])
    for g in range(at["mesh_lists"]):
        column[pl.ds(g * LANES, LANES), :] = jnp.broadcast_to(
            turned[:, g : g + 1], (LANES, LANES)
        )

    def columns(name, start, rows):
        return column[pl.ds(at[name] * LANES + start, rows), :]

    grid_ref[pl.ds(deep - LANES, LANES), :] = jnp.zeros((LANES, grid_count), BF16)
    grid_ref[pl.ds(0, channels), :] = grid_in[...]
    list_hot[...] = pick(columns("lists", 0, 2 * half), 0, grid_count)
    halo_send[...] = nt(list_hot[...], grid_ref[...]).astype(BF16)
    pl.semaphore_wait(barrier, n - 1)
    exchange_start(halo_send, halo_recv, 0)

    w_embed[pl.ds(deep - LANES, LANES), :] = jnp.zeros((LANES, width), BF16)
    w_embed[pl.ds(0, channels), :] = embed_in[...]
    inner = lax.broadcasted_iota(jnp.int32, (n, per, LANES), 1)
    listed = jnp.zeros((n, per, LANES), jnp.int32)
    for j in range(slots):
        g = at["mesh_lists"] + j
        value = jnp.broadcast_to(turned[0:n, g : g + 1], (n, LANES))
        listed = jnp.where(
            lax.shift_right_logical(inner, shift) == j,
            jnp.broadcast_to(value[:, None, :], (n, per, LANES)),
            listed,
        )
    hot_lists[...] = pick(listed.reshape(slabs, LANES), 0, nodes)

    def embed(i, carry):
        rows = pl.ds(pl.multiple_of(i * TILE, TILE), TILE)
        hidden, slope = gate(tn(grid_ref[:, rows], w_embed[...]))
        slope_grid[rows, :] = slope.astype(BF16)
        table[rows, :] = nn(hidden.astype(BF16), w_source[...]).astype(BF16)
        return carry

    lax.fori_loop(0, grid_count // TILE, embed, 0)
    mesh = mesh_ref[...]
    table[pl.ds(grid_count, nodes), :] = nn(mesh, w_target[...]).astype(BF16)

    def enc_own(i, carry):
        start = pl.multiple_of(i * TILE, TILE)
        rows = pl.ds(start, TILE)
        own = pick(columns("enc_target", start, TILE), 0, nodes)
        hot_enc[rows, :] = own
        hot_halo[rows, :] = pick(columns("enc_source", start, TILE), grid_count, 2 * half)
        chosen = jnp.concatenate(
            [pick(columns("enc_source", start, TILE), 0, grid_count), own], axis=1
        )
        pre[rows, :] = nn(chosen, table[...])
        return carry

    lax.fori_loop(0, enc // TILE, enc_own, 0)
    row_enc[...] = spread(index_ref, at["enc_target"], enc // LANES, 0, nodes)
    row_halo[...] = spread(index_ref, at["enc_source"], enc // LANES, grid_count, 2 * half)
    exchange_wait(halo_send, halo_recv, 0)
    hidden, slope = gate(nn(halo_recv[...], w_embed[...]))
    slope_halo[...] = slope.astype(BF16)
    halo[...] = nn(hidden.astype(BF16), w_source[...]).astype(BF16)

    def enc_halo(i, carry):
        rows = pl.ds(pl.multiple_of(i * TILE, TILE), TILE)
        message, slope = gate(pre[rows, :] + nn(hot_halo[rows, :], halo[...]))
        edge[rows, :] = message.astype(BF16)
        slope_enc[rows, :] = slope.astype(BF16)
        return carry

    lax.fori_loop(0, enc // TILE, enc_halo, 0)
    edges = pl.ds(0, enc)
    enc_sum = nn(row_enc[...], edge[edges, :])
    update, slope_node = gate(nn(enc_sum.astype(BF16), w_node[...]))
    latent = (mesh.astype(F32) + update).astype(BF16)
    sender = nn(latent, w_sender[...]).astype(BF16)
    slab_send[...] = (
        packed(nn(hot_lists[...], sender), blocks).reshape(n, per, LANES).astype(BF16)
    )
    scatter_start(slab_send, slab_recv, 0)
    slab_recv[me] = slab_send[me]
    pair[pl.ds(0, nodes), :] = sender
    pair[pl.ds(nodes, nodes), :] = nn(latent, w_receiver[...]).astype(BF16)

    def proc_own(i, carry):
        start = pl.multiple_of(i * TILE, TILE)
        rows = pl.ds(start, TILE)
        own = pick(columns("proc_target", start, TILE), 0, nodes)
        hot_proc[rows, :] = own
        hot_far[rows, :] = pick(columns("proc_source", start, TILE), nodes, slabs, shift)
        chosen = jnp.concatenate(
            [pick(columns("proc_source", start, TILE), 0, nodes), own], axis=1
        )
        pre[rows, :] = nn(chosen, pair[...])
        return carry

    lax.fori_loop(0, proc // TILE, proc_own, 0)
    row_proc[...] = spread(index_ref, at["proc_target"], proc // LANES, 0, nodes)
    row_far[...] = spread(index_ref, at["proc_source"], proc // LANES, nodes, slabs, shift)
    scatter_wait(slab_send, slab_recv, 0)
    arrived = unpacked(slab_recv[...].astype(F32).reshape(slabs, LANES), blocks)

    def proc_far(i, carry):
        rows = pl.ds(pl.multiple_of(i * TILE, TILE), TILE)
        message, slope = gate(pre[rows, :] + nn(hot_far[rows, :], arrived))
        edge[rows, :] = message.astype(BF16)
        slope_proc[rows, :] = slope.astype(BF16)
        return carry

    lax.fori_loop(0, proc // TILE, proc_far, 0)
    proc_sum = nn(row_proc[...], edge[...])
    update, slope = gate(nn(proc_sum.astype(BF16), w_update[...]))
    out_ref[...] = (latent.astype(F32) + update).astype(BF16)
    cotangent = cot_ref[...].astype(F32)
    grad_sum = nt((cotangent * slope).astype(BF16), w_update[...]).astype(BF16)

    def proc_back(i, carry):
        rows = pl.ds(pl.multiple_of(i * TILE, TILE), TILE)
        edge[rows, :] = (
            nn(hot_proc[rows, :], grad_sum) * slope_proc[rows, :].astype(F32)
        ).astype(BF16)
        return carry

    lax.fori_loop(0, proc // TILE, proc_back, 0)
    turn_send[...] = (
        packed(nn(row_far[...], edge[...]), blocks).reshape(n, per, LANES).astype(BF16)
    )
    scatter_start(turn_send, turn_recv, 1)
    turn_recv[me] = turn_send[me]
    grad_receiver = nn(row_proc[...], edge[...]).astype(BF16)
    grad_latent = cotangent + nt(grad_receiver, w_receiver[...])
    grad_sender = nn(spread(index_ref, at["proc_source"], proc // LANES, 0, nodes), edge[...])
    scatter_wait(turn_send, turn_recv, 1)
    grad_sender = grad_sender + tn(
        hot_lists[...], unpacked(turn_recv[...].astype(F32).reshape(slabs, LANES), blocks)
    )
    grad_latent = grad_latent + nt(grad_sender.astype(BF16), w_sender[...])
    grad_latent = grad_latent.astype(BF16).astype(F32)
    grad_sum = nt((grad_latent * slope_node).astype(BF16), w_node[...]).astype(BF16)

    def enc_back(i, carry):
        rows = pl.ds(pl.multiple_of(i * TILE, TILE), TILE)
        edge[rows, :] = (
            nn(hot_enc[rows, :], grad_sum) * slope_enc[rows, :].astype(F32)
        ).astype(BF16)
        return carry

    lax.fori_loop(0, enc // TILE, enc_back, 0)
    grad_far = nt(nn(row_halo[...], edge[edges, :]).astype(BF16), w_source[...])
    grad_far = (grad_far * slope_halo[...].astype(F32)).astype(BF16)
    back_send[...] = nt(grad_far, w_embed[...]).astype(BF16)
    exchange_start(back_send, back, 1)
    grad_target = nn(row_enc[...], edge[edges, :]).astype(BF16)
    grad_mesh_ref[...] = (grad_latent + nt(grad_target, w_target[...])).astype(BF16)

    def grid_own(i, carry):
        start = pl.multiple_of(i * TILE, TILE)
        rows = pl.ds(start, TILE)
        total = nn(spread(index_ref, at["enc_source"], enc // LANES, start, TILE), edge[edges, :])
        grad_hidden = nt(total.astype(BF16), w_source[...])
        grad_pre = (grad_hidden * slope_grid[rows, :].astype(F32)).astype(BF16)
        grad_part[:, rows] = nt(w_embed[...], grad_pre)
        return carry

    lax.fori_loop(0, grid_count // TILE, grid_own, 0)
    exchange_wait(back_send, back, 1)
    total = grad_part[...] + tn(back[...], list_hot[...])
    grad_grid_ref[...] = total[0:channels, :].astype(BF16)


def local(
    grid_input,
    mesh_init,
    cotangent,
    grid_lists,
    encoder_source,
    encoder_target,
    mesh_lists,
    mesh_source,
    mesh_target,
    w_embed,
    w_source,
    w_target,
    w_node,
    w_sender,
    w_receiver,
    w_update,
):
    n = lax.axis_size("band")
    channels, grid_count = grid_input.shape
    nodes, width = mesh_init.shape
    half = grid_lists.shape[1]
    enc = encoder_source.shape[0]
    proc = mesh_source.shape[0]
    slots = mesh_lists.shape[1]
    per = slots * (width // LANES)
    slabs = n * per
    deep = -(-channels // LANES) * LANES
    at = {}
    used = 0
    for name, groups in (
        ("enc_source", enc // LANES),
        ("enc_target", enc // LANES),
        ("proc_source", proc // LANES),
        ("proc_target", proc // LANES),
        ("lists", 2 * half // LANES),
        ("mesh_lists", slots),
    ):
        at[name] = used
        used += groups
    most = max(enc, proc)
    vmem = pl.BlockSpec(memory_space=pltpu.VMEM)
    half_vmem = lambda *shape: pltpu.VMEM(shape, BF16)
    return pl.pallas_call(
        functools.partial(kernel, n, at),
        out_shape=(
            jax.ShapeDtypeStruct((nodes, width), BF16),
            jax.ShapeDtypeStruct((channels, grid_count), BF16),
            jax.ShapeDtypeStruct((nodes, width), BF16),
        ),
        in_specs=[vmem] * 16,
        out_specs=(vmem, vmem, vmem),
        scratch_shapes=[
            pltpu.VMEM((-(-used // 8) * 8, LANES), jnp.int32),
            pltpu.VMEM((used * LANES, LANES), jnp.int32),
            half_vmem(deep, grid_count),
            half_vmem(deep, width),
            half_vmem(2 * half, grid_count),
            half_vmem(grid_count + nodes, width),
            half_vmem(2 * half, width),
            half_vmem(2 * half, deep),
            half_vmem(2 * half, deep),
            half_vmem(2 * half, deep),
            half_vmem(2 * half, deep),
            pltpu.VMEM((most, width), F32),
            half_vmem(most, width),
            pltpu.VMEM((deep, grid_count), F32),
            half_vmem(grid_count, width),
            half_vmem(2 * half, width),
            half_vmem(enc, width),
            half_vmem(proc, width),
            half_vmem(2 * nodes, width),
            half_vmem(enc, 2 * half),
            half_vmem(enc, nodes),
            half_vmem(nodes, enc),
            half_vmem(2 * half, enc),
            half_vmem(proc, slabs),
            half_vmem(proc, nodes),
            half_vmem(nodes, proc),
            half_vmem(slabs, proc),
            half_vmem(slabs, nodes),
            half_vmem(n, per, LANES),
            half_vmem(n, per, LANES),
            half_vmem(n, per, LANES),
            half_vmem(n, per, LANES),
            pltpu.SemaphoreType.DMA((2, 2, 2)),
            pltpu.SemaphoreType.DMA((2, 2)),
        ],
        compiler_params=pltpu.CompilerParams(
            collective_id=0, has_side_effects=True, vmem_limit_bytes=56 * 1024 * 1024
        ),
    )(
        encoder_source.reshape(1, -1),
        encoder_target.reshape(1, -1),
        mesh_source.reshape(1, -1),
        mesh_target.reshape(1, -1),
        grid_lists,
        mesh_lists.T,
        grid_input,
        mesh_init,
        cotangent,
        w_embed,
        w_source,
        w_target,
        w_node,
        w_sender,
        w_receiver,
        w_update,
    )


def solution(mesh):
    placed = (
        P(None, "band"),
        P("band", None),
        P("band", None),
        P("band", None),
        P("band"),
        P("band"),
        P("band", None),
        P("band"),
        P("band"),
        P(),
        P(),
        P(),
        P(),
        P(),
        P(),
        P(),
    )
    return jax.shard_map(
        local,
        mesh=mesh,
        in_specs=placed,
        out_specs=(P("band", None), P(None, "band"), P("band", None)),
        check_vma=False,
    )
```

```python
import functools

import jax
import jax.numpy as jnp
from jax import lax
from jax.experimental import pallas as pl
from jax.experimental.pallas import tpu as pltpu
from jax.sharding import PartitionSpec as P

F32 = jnp.float32
BF16 = jnp.bfloat16
MESH = pl.DeviceIdType.MESH
LANES = 128
TILE = 512


def nn(left, right):
    return jnp.dot(left, right, preferred_element_type=F32)


def nt(left, right):
    return lax.dot_general(left, right, (((1,), (1,)), ((), ())), preferred_element_type=F32)


def tn(left, right):
    return lax.dot_general(left, right, (((0,), (0,)), ((), ())), preferred_element_type=F32)


def gate(values):
    sigmoid = 0.5 * jnp.tanh(0.5 * values) + 0.5
    out = values * sigmoid
    return out, sigmoid + out - out * sigmoid


def pick(column, base, width, shift=0):
    lane = lax.broadcasted_iota(jnp.int32, column.shape, 1)
    parts = [
        jnp.where(column == lax.shift_right_logical(lane + k, shift) + base, 1.0, 0.0).astype(BF16)
        for k in range(0, width, LANES)
    ]
    return jnp.concatenate(parts, axis=1)


def spread(index_ref, first, groups, base, rows, shift=0):
    row = lax.broadcasted_iota(jnp.int32, (rows, LANES), 0)
    row = lax.shift_right_logical(row, shift) + base
    parts = [
        jnp.where(index_ref[g : g + 1, :] == row, 1.0, 0.0).astype(BF16)
        for g in range(first, first + groups)
    ]
    return jnp.concatenate(parts, axis=1)


def block_rows(shape, blocks):
    return lax.broadcasted_iota(jnp.int32, shape, 0) & (blocks - 1)


def packed(full, blocks):
    which = block_rows((full.shape[0], LANES), blocks)
    out = full[:, :LANES]
    for c in range(1, blocks):
        out = jnp.where(which == c, full[:, c * LANES : (c + 1) * LANES], out)
    return out


def unpacked(part, blocks):
    which = block_rows(part.shape, blocks)
    return jnp.concatenate(
        [jnp.where(which == c, part, 0.0).astype(BF16) for c in range(blocks)], axis=1
    )


def kernel(
    n,
    at,
    enc_source_ref,
    enc_target_ref,
    proc_source_ref,
    proc_target_ref,
    lists_ref,
    mesh_lists_ref,
    grid_in,
    mesh_ref,
    cot_ref,
    embed_in,
    w_source,
    w_target,
    w_node,
    w_sender,
    w_receiver,
    w_update,
    out_ref,
    grad_grid_ref,
    grad_mesh_ref,
    index_ref,
    column,
    grid_ref,
    w_embed,
    list_hot,
    table,
    halo,
    halo_send,
    halo_recv,
    back,
    back_send,
    pre,
    edge,
    grad_part,
    slope_grid,
    slope_halo,
    slope_enc,
    slope_proc,
    pair,
    hot_halo,
    hot_enc,
    row_enc,
    row_halo,
    hot_far,
    hot_proc,
    row_proc,
    row_far,
    hot_lists,
    slab_send,
    slab_recv,
    turn_send,
    turn_recv,
    halo_sems,
    slab_sems,
):
    me = lax.axis_index("band")
    channels, grid_count = grid_in.shape
    nodes, width = mesh_ref.shape
    half = halo.shape[0] // 2
    enc = slope_enc.shape[0]
    proc = slope_proc.shape[0]
    slots = mesh_lists_ref.shape[0]
    blocks = width // LANES
    shift = blocks.bit_length() - 1
    per = slots * blocks
    slabs = n * per
    deep = grid_ref.shape[0]

    def exchange(source, target, k, kind):
        device = lax.rem(me + (n - 1 if k == 0 else 1), n)
        return pltpu.make_async_remote_copy(
            src_ref=source.at[pl.ds(k * half, half)],
            dst_ref=target.at[pl.ds((1 - k) * half, half)],
            send_sem=halo_sems.at[kind, 0, k],
            recv_sem=halo_sems.at[kind, 1, k],
            device_id=(device,),
            device_id_type=MESH,
        )

    def exchange_start(source, target, kind):
        @pl.when(me > 0)
        def _():
            exchange(source, target, 0, kind).start()

        @pl.when(me < n - 1)
        def _():
            exchange(source, target, 1, kind).start()

    def exchange_wait(source, target, kind):
        @pl.when(me < n - 1)
        def _():
            exchange(source, target, 0, kind).wait_recv()
            exchange(source, target, 1, kind).wait_send()

        @pl.when(me > 0)
        def _():
            exchange(source, target, 1, kind).wait_recv()
            exchange(source, target, 0, kind).wait_send()

    def scatter_start(source, target, kind):
        def send(k, carry):
            other = lax.rem(me + k, n)
            pltpu.make_async_remote_copy(
                src_ref=source.at[other],
                dst_ref=target.at[me],
                send_sem=slab_sems.at[kind, 0],
                recv_sem=slab_sems.at[kind, 1],
                device_id=(other,),
                device_id_type=MESH,
            ).start()
            return carry

        lax.fori_loop(1, n, send, 0)

    def scatter_wait(source, target, kind):
        whole_source = source.at[pl.ds(0, n - 1)]
        whole_target = target.at[pl.ds(0, n - 1)]
        pltpu.make_async_copy(whole_source, whole_target, slab_sems.at[kind, 0]).wait()
        pltpu.make_async_copy(whole_source, whole_target, slab_sems.at[kind, 1]).wait()

    @pl.when(me == 0)
    def _():
        halo_recv[pl.ds(0, half), :] = jnp.zeros((half, deep), BF16)
        back[pl.ds(0, half), :] = jnp.zeros((half, deep), BF16)

    @pl.when(me == n - 1)
    def _():
        halo_recv[pl.ds(half, half), :] = jnp.zeros((half, deep), BF16)
        back[pl.ds(half, half), :] = jnp.zeros((half, deep), BF16)

    barrier = pltpu.get_barrier_semaphore()

    def greet(k, carry):
        pl.semaphore_signal(
            barrier, inc=1, device_id=(lax.rem(me + k, n),), device_id_type=MESH
        )
        return carry

    lax.fori_loop(1, n, greet, 0)

    index_ref[...] = jnp.zeros_like(index_ref)
    for name, ref in (
        ("enc_source", enc_source_ref),
        ("enc_target", enc_target_ref),
        ("proc_source", proc_source_ref),
        ("proc_target", proc_target_ref),
    ):
        for g in range(ref.shape[0] // LANES):
            index_ref[at[name] + g : at[name] + g + 1, :] = ref[pl.ds(g * LANES, LANES)].reshape(
                1, LANES
            )
    each = half // LANES
    for g in range(2 * each):
        index_ref[at["lists"] + g : at["lists"] + g + 1, :] = lists_ref[
            g // each : g // each + 1, g % each * LANES : (g % each + 1) * LANES
        ]
    for j in range(slots):
        index_ref[at["mesh_lists"] + j : at["mesh_lists"] + j + 1, 0:n] = mesh_lists_ref[
            j : j + 1, :
        ]
    turned = jnp.transpose(index_ref[...])
    for g in range(at["mesh_lists"]):
        column[pl.ds(g * LANES, LANES), :] = jnp.broadcast_to(
            turned[:, g : g + 1], (LANES, LANES)
        )

    def columns(name, start, rows):
        return column[pl.ds(at[name] * LANES + start, rows), :]

    grid_ref[pl.ds(deep - LANES, LANES), :] = jnp.zeros((LANES, grid_count), BF16)
    grid_ref[pl.ds(0, channels), :] = grid_in[...]
    list_hot[...] = pick(columns("lists", 0, 2 * half), 0, grid_count)
    halo_send[...] = nt(list_hot[...], grid_ref[...]).astype(BF16)
    pl.semaphore_wait(barrier, n - 1)
    exchange_start(halo_send, halo_recv, 0)

    w_embed[pl.ds(deep - LANES, LANES), :] = jnp.zeros((LANES, width), BF16)
    w_embed[pl.ds(0, channels), :] = embed_in[...]
    inner = lax.broadcasted_iota(jnp.int32, (n, per, LANES), 1)
    listed = jnp.zeros((n, per, LANES), jnp.int32)
    for j in range(slots):
        g = at["mesh_lists"] + j
        value = jnp.broadcast_to(turned[0:n, g : g + 1], (n, LANES))
        listed = jnp.where(
            lax.shift_right_logical(inner, shift) == j,
            jnp.broadcast_to(value[:, None, :], (n, per, LANES)),
            listed,
        )
    hot_lists[...] = pick(listed.reshape(slabs, LANES), 0, nodes)

    def embed(i, carry):
        rows = pl.ds(pl.multiple_of(i * TILE, TILE), TILE)
        hidden, slope = gate(tn(grid_ref[:, rows], w_embed[...]))
        slope_grid[rows, :] = slope.astype(BF16)
        table[rows, :] = nn(hidden.astype(BF16), w_source[...]).astype(BF16)
        return carry

    lax.fori_loop(0, grid_count // TILE, embed, 0)
    mesh = mesh_ref[...]
    table[pl.ds(grid_count, nodes), :] = nn(mesh, w_target[...]).astype(BF16)

    def enc_own(i, carry):
        start = pl.multiple_of(i * TILE, TILE)
        rows = pl.ds(start, TILE)
        own = pick(columns("enc_target", start, TILE), 0, nodes)
        hot_enc[rows, :] = own
        hot_halo[rows, :] = pick(columns("enc_source", start, TILE), grid_count, 2 * half)
        chosen = jnp.concatenate(
            [pick(columns("enc_source", start, TILE), 0, grid_count), own], axis=1
        )
        pre[rows, :] = nn(chosen, table[...])
        return carry

    lax.fori_loop(0, enc // TILE, enc_own, 0)
    row_enc[...] = spread(index_ref, at["enc_target"], enc // LANES, 0, nodes)
    row_halo[...] = spread(index_ref, at["enc_source"], enc // LANES, grid_count, 2 * half)
    exchange_wait(halo_send, halo_recv, 0)
    hidden, slope = gate(nn(halo_recv[...], w_embed[...]))
    slope_halo[...] = slope.astype(BF16)
    halo[...] = nn(hidden.astype(BF16), w_source[...]).astype(BF16)

    def enc_halo(i, carry):
        rows = pl.ds(pl.multiple_of(i * TILE, TILE), TILE)
        message, slope = gate(pre[rows, :] + nn(hot_halo[rows, :], halo[...]))
        edge[rows, :] = message.astype(BF16)
        slope_enc[rows, :] = slope.astype(BF16)
        return carry

    lax.fori_loop(0, enc // TILE, enc_halo, 0)
    edges = pl.ds(0, enc)
    enc_sum = nn(row_enc[...], edge[edges, :])
    update, slope_node = gate(nn(enc_sum.astype(BF16), w_node[...]))
    latent = (mesh.astype(F32) + update).astype(BF16)
    sender = nn(latent, w_sender[...]).astype(BF16)
    slab_send[...] = (
        packed(nn(hot_lists[...], sender), blocks).reshape(n, per, LANES).astype(BF16)
    )
    scatter_start(slab_send, slab_recv, 0)
    slab_recv[me] = slab_send[me]
    pair[pl.ds(0, nodes), :] = sender
    pair[pl.ds(nodes, nodes), :] = nn(latent, w_receiver[...]).astype(BF16)

    def proc_own(i, carry):
        start = pl.multiple_of(i * TILE, TILE)
        rows = pl.ds(start, TILE)
        own = pick(columns("proc_target", start, TILE), 0, nodes)
        hot_proc[rows, :] = own
        hot_far[rows, :] = pick(columns("proc_source", start, TILE), nodes, slabs, shift)
        chosen = jnp.concatenate(
            [pick(columns("proc_source", start, TILE), 0, nodes), own], axis=1
        )
        pre[rows, :] = nn(chosen, pair[...])
        return carry

    lax.fori_loop(0, proc // TILE, proc_own, 0)
    row_proc[...] = spread(index_ref, at["proc_target"], proc // LANES, 0, nodes)
    row_far[...] = spread(index_ref, at["proc_source"], proc // LANES, nodes, slabs, shift)
    scatter_wait(slab_send, slab_recv, 0)
    arrived = unpacked(slab_recv[...].astype(F32).reshape(slabs, LANES), blocks)

    def proc_far(i, carry):
        rows = pl.ds(pl.multiple_of(i * TILE, TILE), TILE)
        message, slope = gate(pre[rows, :] + nn(hot_far[rows, :], arrived))
        edge[rows, :] = message.astype(BF16)
        slope_proc[rows, :] = slope.astype(BF16)
        return carry

    lax.fori_loop(0, proc // TILE, proc_far, 0)
    proc_sum = nn(row_proc[...], edge[...])
    update, slope = gate(nn(proc_sum.astype(BF16), w_update[...]))
    out_ref[...] = (latent.astype(F32) + update).astype(BF16)
    cotangent = cot_ref[...].astype(F32)
    grad_sum = nt((cotangent * slope).astype(BF16), w_update[...]).astype(BF16)

    def proc_back(i, carry):
        rows = pl.ds(pl.multiple_of(i * TILE, TILE), TILE)
        edge[rows, :] = (
            nn(hot_proc[rows, :], grad_sum) * slope_proc[rows, :].astype(F32)
        ).astype(BF16)
        return carry

    lax.fori_loop(0, proc // TILE, proc_back, 0)
    turn_send[...] = (
        packed(nn(row_far[...], edge[...]), blocks).reshape(n, per, LANES).astype(BF16)
    )
    scatter_start(turn_send, turn_recv, 1)
    turn_recv[me] = turn_send[me]
    grad_receiver = nn(row_proc[...], edge[...]).astype(BF16)
    grad_latent = cotangent + nt(grad_receiver, w_receiver[...])
    grad_sender = nn(spread(index_ref, at["proc_source"], proc // LANES, 0, nodes), edge[...])
    scatter_wait(turn_send, turn_recv, 1)
    grad_sender = grad_sender + tn(
        hot_lists[...], unpacked(turn_recv[...].astype(F32).reshape(slabs, LANES), blocks)
    )
    grad_latent = grad_latent + nt(grad_sender.astype(BF16), w_sender[...])
    grad_latent = grad_latent.astype(BF16).astype(F32)
    grad_sum = nt((grad_latent * slope_node).astype(BF16), w_node[...]).astype(BF16)

    def enc_back(i, carry):
        rows = pl.ds(pl.multiple_of(i * TILE, TILE), TILE)
        edge[rows, :] = (
            nn(hot_enc[rows, :], grad_sum) * slope_enc[rows, :].astype(F32)
        ).astype(BF16)
        return carry

    lax.fori_loop(0, enc // TILE, enc_back, 0)
    grad_far = nt(nn(row_halo[...], edge[edges, :]).astype(BF16), w_source[...])
    grad_far = (grad_far * slope_halo[...].astype(F32)).astype(BF16)
    back_send[...] = nt(grad_far, w_embed[...]).astype(BF16)
    exchange_start(back_send, back, 1)
    grad_target = nn(row_enc[...], edge[edges, :]).astype(BF16)
    grad_mesh_ref[...] = (grad_latent + nt(grad_target, w_target[...])).astype(BF16)

    def grid_own(i, carry):
        start = pl.multiple_of(i * TILE, TILE)
        rows = pl.ds(start, TILE)
        total = nn(spread(index_ref, at["enc_source"], enc // LANES, start, TILE), edge[edges, :])
        grad_hidden = nt(total.astype(BF16), w_source[...])
        grad_pre = (grad_hidden * slope_grid[rows, :].astype(F32)).astype(BF16)
        grad_part[:, rows] = nt(w_embed[...], grad_pre)
        return carry

    lax.fori_loop(0, grid_count // TILE, grid_own, 0)
    exchange_wait(back_send, back, 1)
    total = grad_part[...] + tn(back[...], list_hot[...])
    grad_grid_ref[...] = total[0:channels, :].astype(BF16)


def hand_over(first, second, third, first_out, second_out, third_out):
    first_out[...] = first[...]
    second_out[...] = second[...]
    third_out[...] = third[...]


def local(
    grid_input,
    mesh_init,
    cotangent,
    grid_lists,
    encoder_source,
    encoder_target,
    mesh_lists,
    mesh_source,
    mesh_target,
    w_embed,
    w_source,
    w_target,
    w_node,
    w_sender,
    w_receiver,
    w_update,
):
    n = lax.axis_size("band")
    channels, grid_count = grid_input.shape
    nodes, width = mesh_init.shape
    half = grid_lists.shape[1]
    enc = encoder_source.shape[0]
    proc = mesh_source.shape[0]
    slots = mesh_lists.shape[1]
    per = slots * (width // LANES)
    slabs = n * per
    deep = -(-channels // LANES) * LANES
    at = {}
    used = 0
    for name, groups in (
        ("enc_source", enc // LANES),
        ("enc_target", enc // LANES),
        ("proc_source", proc // LANES),
        ("proc_target", proc // LANES),
        ("lists", 2 * half // LANES),
        ("mesh_lists", slots),
    ):
        at[name] = used
        used += groups
    most = max(enc, proc)
    vmem = pl.BlockSpec(memory_space=pltpu.VMEM)
    half_vmem = lambda *shape: pltpu.VMEM(shape, BF16)
    results = pl.pallas_call(
        functools.partial(kernel, n, at),
        out_shape=(
            jax.ShapeDtypeStruct((nodes, width), BF16),
            jax.ShapeDtypeStruct((channels, grid_count), BF16),
            jax.ShapeDtypeStruct((nodes, width), BF16),
        ),
        in_specs=[vmem] * 16,
        out_specs=(vmem, vmem, vmem),
        scratch_shapes=[
            pltpu.VMEM((-(-used // 8) * 8, LANES), jnp.int32),
            pltpu.VMEM((used * LANES, LANES), jnp.int32),
            half_vmem(deep, grid_count),
            half_vmem(deep, width),
            half_vmem(2 * half, grid_count),
            half_vmem(grid_count + nodes, width),
            half_vmem(2 * half, width),
            half_vmem(2 * half, deep),
            half_vmem(2 * half, deep),
            half_vmem(2 * half, deep),
            half_vmem(2 * half, deep),
            pltpu.VMEM((most, width), F32),
            half_vmem(most, width),
            pltpu.VMEM((deep, grid_count), F32),
            half_vmem(grid_count, width),
            half_vmem(2 * half, width),
            half_vmem(enc, width),
            half_vmem(proc, width),
            half_vmem(2 * nodes, width),
            half_vmem(enc, 2 * half),
            half_vmem(enc, nodes),
            half_vmem(nodes, enc),
            half_vmem(2 * half, enc),
            half_vmem(proc, slabs),
            half_vmem(proc, nodes),
            half_vmem(nodes, proc),
            half_vmem(slabs, proc),
            half_vmem(slabs, nodes),
            half_vmem(n, per, LANES),
            half_vmem(n, per, LANES),
            half_vmem(n, per, LANES),
            half_vmem(n, per, LANES),
            pltpu.SemaphoreType.DMA((2, 2, 2)),
            pltpu.SemaphoreType.DMA((2, 2)),
        ],
        compiler_params=pltpu.CompilerParams(
            collective_id=0, has_side_effects=True, vmem_limit_bytes=56 * 1024 * 1024
        ),
    )(
        encoder_source,
        encoder_target,
        mesh_source,
        mesh_target,
        grid_lists,
        mesh_lists.T,
        grid_input,
        mesh_init,
        cotangent,
        w_embed,
        w_source,
        w_target,
        w_node,
        w_sender,
        w_receiver,
        w_update,
    )
    return pl.pallas_call(
        hand_over,
        out_shape=tuple(jax.ShapeDtypeStruct(r.shape, r.dtype) for r in results),
        in_specs=[vmem] * 3,
        out_specs=(vmem, vmem, vmem),
    )(*results)


def solution(mesh):
    placed = (
        P(None, "band"),
        P("band", None),
        P("band", None),
        P("band", None),
        P("band"),
        P("band"),
        P("band", None),
        P("band"),
        P("band"),
        P(),
        P(),
        P(),
        P(),
        P(),
        P(),
        P(),
    )
    return jax.shard_map(
        local,
        mesh=mesh,
        in_specs=placed,
        out_specs=(P("band", None), P(None, "band"), P("band", None)),
        check_vma=False,
    )
```
